32 devices in a mesh: dp: 8 (over z, x), expert: 4 (over y, core).
Axes of the slice: x: 2, y: 2, z: 4, core: 2. Of those that a mesh axis runs over, the one named last changes fastest.
Arguments:
- layer_in: bfloat16 [8192, 1024], P(('dp', 'expert')), may hold values from -6 to 6
- body_of: int32 [8192], P(('dp', 'expert')), may hold values from 0 to 5, as said below
- expert_of: int32 [8192, 1], P(('dp', 'expert')), may hold values from 0 to 7; in each aligned block of 256 rows (0 to 255, 256 to 511, ...) at most 48 rows name the same one
- w_qkv: bfloat16 [1024, 1536], replicated, may hold values from -0.1875 to 0.1875
- w_o: bfloat16 [1024, 512], replicated, may hold values from -0.25 to 0.25
- w_up: bfloat16 [8, 1024, 1024], P('expert', None, 'dp'), may hold values from -0.1875 to 0.1875
- w_down: bfloat16 [8, 1024, 1024], P('expert', 'dp'), may hold values from -0.1875 to 0.1875
- d_out: bfloat16 [8192, 1024], P(('dp', 'expert')), may hold values from -6 to 6
Outputs:
- out: bfloat16 [8192, 1024], P(('dp', 'expert'))
- grad_input: bfloat16 [8192, 1024], P(('dp', 'expert'))
- grad_qkv: float32 [1024, 1536], P(('dp', 'expert'))
- grad_o: float32 [1024, 512], P(('dp', 'expert'))
- grad_up: float32 [8, 1024, 1024], P('expert', None, 'dp')
- grad_down: float32 [8, 1024, 1024], P('expert', 'dp')
The draws below stay inside these ranges and needn't reach their ends.
Inputs may be any that keep to these rules, and one draw needn't show every extreme that they name: `body_of`: within each device's 256 rows the ids start at 0 and rise by one at each new body; every body has 16 to 128 tokens, no body crosses a multiple of 128 rows of its device, no block of 128 rows holds more than 3 bodies, and some device holds 3 bodies in each of its blocks. `expert_of`: in the 256 rows of one device no expert is named more than 48 times, a bound that some block reaches.
All inputs are finite; a program needn't handle non-finite values.
Results may differ from the reference program's by a relative error of at most 0.014.
Values may be sent and summed in bfloat16 or wider, within the bound.
A program may use at most 128 MiB of HBM per device.

```python
import math
import jax
import jax.numpy as jnp
import numpy as np
from jax import lax

D = 1024
HEADS = 8
HD = 64
FF = 1024
TOK_DEV = 256
EXPERTS = 8
CAP = 48
TOKENS = 8192
N_DP = 8
N_EXPERT = 4


def draw_body_of(key, part):
    blocks = TOKENS // 128
    devices = TOKENS // TOK_DEV
    keys = jax.random.split(key, 5)
    count = jax.random.randint(keys[0], (blocks,), 1, 4)
    per_device = TOK_DEV // 128
    chosen = jax.random.randint(keys[4], (), 0, devices)
    full_device = jnp.arange(blocks) // per_device == chosen
    count = jnp.where(full_device, 3, count)
    single = jax.random.randint(keys[1], (blocks,), 16, 113)
    lower = jax.random.randint(keys[2], (blocks,), 16, 57)
    spread = jax.random.randint(keys[3], (blocks,), 0, 1 << 20)
    upper = lower + 16 + spread % (97 - lower)
    position = jnp.arange(128)[None, :]
    two_parts = (count[:, None] == 2) & (position == single[:, None])
    three_parts = (count[:, None] == 3) & ((position == lower[:, None]) | (position == upper[:, None]))
    begins = ((position == 0) | two_parts | three_parts).astype(jnp.int32)
    begins = begins.reshape(TOKENS // TOK_DEV, TOK_DEV)
    return (jnp.cumsum(begins, axis=1) - 1).reshape(TOKENS).astype(jnp.int32)


def level_of(own_key, extent, pieces, low, high):
    def one(axis_at, shards_of):
        heights = jax.random.uniform(jax.random.fold_in(jax.random.fold_in(own_key, 6), axis_at), (shards_of,), jnp.float32, low / len(pieces), high / len(pieces))
        return jnp.repeat(jnp.exp(heights), extent[axis_at] // shards_of).reshape((-1,) + (1,) * (len(extent) - axis_at - 1))

    factor_of = one(*pieces[0])
    for cut in pieces[1:]:
        factor_of = factor_of * one(*cut)
    return factor_of


def deal_out(stream_key, own, number, rows, amount, top, most, slope):
    sequence = jax.random.permutation(stream_key, amount)
    heavy_load, ordinary = shares(amount, rows * top, most, slope, True), shares(amount, rows * top, most, slope, False)
    places = jnp.arange(amount)

    def named(lengths, rotation):
        used = int((lengths > 0).sum())
        fixed = max(1, used // 4)
        moved = fixed + (places - fixed + rotation * (used - fixed)) % max(1, amount - fixed)
        return jnp.zeros((amount,), jnp.int32).at[sequence[jnp.where(places < fixed, places, moved)]].set(jnp.asarray(lengths, jnp.int32))

    lengths = jnp.where(number % 4 == 0, named(heavy_load, number // 4), named(ordinary, number - number // 4 - 1))
    mixed = jax.random.permutation(jax.random.fold_in(own, 3), amount)
    source_of, taker = mixed[0:amount // 2 * 2:2], mixed[1:amount // 2 * 2:2]
    slack = jnp.minimum(lengths[source_of] - 1, most - lengths[taker]) // 2
    slack = jnp.where((source_of == sequence[0]) | (taker == sequence[0]) | (lengths[taker] == 0), 0, jnp.maximum(slack, 0))
    moved = jax.random.randint(jax.random.fold_in(own, 4), (amount // 2,), 0, 1 << 20) % (slack + 1)
    lengths = lengths.at[source_of].add(-moved).at[taker].add(moved)
    items = jnp.searchsorted(jnp.cumsum(lengths), jnp.arange(rows * top), side="right").astype(jnp.int32)
    table = items.reshape(top, rows).T
    table = table[jax.random.permutation(jax.random.fold_in(own, 1), rows)]
    rotation = jax.random.randint(jax.random.fold_in(own, 2), (rows, 1), 0, top)
    return jnp.take_along_axis(table, (jnp.arange(top)[None, :] + rotation) % top, axis=1)


def shares(count, total, reach, skew, full):
    loads = [(1 << 20) // math.isqrt(rank ** skew) + 1 for rank in range(1, count + 1)]
    largest = reach if full else min(reach, max(-(-total // count), total * loads[0] // sum(loads)))
    least = 1 if total - largest >= count - 1 else 0
    counts, surplus = [largest] + [least] * (count - 1), total - largest - least * (count - 1)
    while surplus > 0:
        free = [i for i in range(1, count) if counts[i] < largest] or [i for i in range(1, count) if counts[i] < reach]
        whole, budget = sum([loads[i] for i in free]), surplus
        for i in free:
            extra = min(reach - counts[i], max(1, budget * loads[i] // whole), surplus)
            counts[i] = counts[i] + extra
            surplus = surplus - extra
    return np.array(counts)


def normal_values(stream_key, dims, scale, limit, shards=(), held_as=jnp.bfloat16):
    array = jax.random.normal(stream_key, dims, jnp.float32) * scale
    if len(shards) > 0:
        array = level_of(stream_key, dims, shards, -0.22, 0.18) * array
    return jnp.clip(array, min=-limit, max=limit).astype(held_as)


def setup_inputs(seed: int = 0) -> dict:
    splits = jax.random.split(jax.random.key(seed), 9)
    layer_in = normal_values(splits[0], (TOKENS, D), 1.0, 6.0, ((0, 32),))
    body_of = draw_body_of(jax.random.fold_in(splits[8], 71), 0)
    expert_of_keys = jax.random.split(jax.random.fold_in(splits[2], 1), TOKENS // TOK_DEV)
    expert_of_turns = jax.random.permutation(jax.random.fold_in(splits[2], 3), TOKENS // TOK_DEV)
    expert_of = jax.vmap(lambda own, number: deal_out(jax.random.fold_in(splits[2], 2), own, number, TOK_DEV, EXPERTS, 1, CAP, 2))(expert_of_keys, expert_of_turns).reshape((TOKENS, 1))
    w_qkv = normal_values(splits[3], (D, 3 * HEADS * HD), D ** -0.5, 0.1875)
    w_o = normal_values(splits[4], (D, HEADS * HD), (HEADS * HD) ** -0.5, 0.25)
    w_up = normal_values(splits[5], (EXPERTS, D, FF), D ** -0.5, 0.1875, ((0, 4), (2, 8)))
    w_down = normal_values(splits[6], (EXPERTS, FF, D), FF ** -0.5, 0.1875, ((0, 4), (1, 8)))
    d_out = normal_values(splits[7], (TOKENS, D), 1.0, 6.0, ((0, 32),))
    return dict(layer_in=layer_in, body_of=body_of, expert_of=expert_of, w_qkv=w_qkv, w_o=w_o, w_up=w_up, w_down=w_down, d_out=d_out)


EPSILON = 1e-06

def rms_norm(values):
    scale = lax.rsqrt(lax.optimization_barrier(jnp.mean(values * values, axis=-1, keepdims=True)) + EPSILON)
    return (values * scale).astype(jnp.bfloat16)

def gelu_tanh(values):
    return jax.nn.gelu(values, approximate=True)

def gelu_back(pre_act, cotangent):
    return jax.vjp(gelu_tanh, pre_act)[1](cotangent)[0]

def row_contract(left, right):
    return lax.dot_general(left, right, (((0,), (0,)), ((), ())), preferred_element_type=jnp.float32)

def col_contract(left, right):
    return lax.dot_general(left, right, (((1,), (1,)), ((), ())), preferred_element_type=jnp.float32)

def attention_core(packed, labels_row):
    rows = packed.shape[0]
    blocks = rows // 128
    width = packed.shape[1] // 3
    heads = width // HD
    parts = packed.reshape(blocks, 128, 3, heads, HD).astype(jnp.float32)
    query = parts[:, :, 0]
    keys = parts[:, :, 1]
    values = parts[:, :, 2]
    scores = jnp.einsum('bqhc,bkhc->bhqk', query, keys) * HD ** (-0.5)
    labels = labels_row.reshape(blocks, 128)
    same = (labels[:, :, None] == labels[:, None, :])[:, None]
    weights = jnp.where(same, jnp.exp(scores), 0.0)
    probs = (weights / lax.optimization_barrier(jnp.sum(weights, axis=-1, keepdims=True))).astype(jnp.bfloat16)
    mixed = jnp.einsum('bhqk,bkhc->bqhc', probs.astype(jnp.float32), values)
    return mixed.astype(jnp.bfloat16).reshape(rows, width)

def reference(layer_in, body_of, expert_of, w_qkv, w_o, w_up, w_down, d_out):
    devices = N_DP * N_EXPERT
    x_dev = layer_in.reshape(devices, TOK_DEV, D)
    label_dev = body_of.reshape(devices, TOK_DEV)
    cot_dev = d_out.reshape(devices, TOK_DEV, D)

    def front(args):
        x_part, label_part = args
        normed = rms_norm(x_part.astype(jnp.float32))
        packed = jnp.dot(normed, w_qkv, preferred_element_type=jnp.float32).astype(jnp.bfloat16)
        mixed = attention_core(packed, label_part)
        resid = (x_part.astype(jnp.float32) + col_contract(mixed, w_o)).astype(jnp.bfloat16)
        return (resid, rms_norm(resid.astype(jnp.float32)))
    resid, inner = lax.map(front, (x_dev, label_dev))
    expert_ids = expert_of[:, 0].reshape(devices, TOK_DEV)
    onehot = (expert_ids[:, :, None] == jnp.arange(EXPERTS, dtype=jnp.int32)[None, None, :]).astype(jnp.int32)
    ranks = lax.optimization_barrier(jnp.sum(jnp.cumsum(onehot, axis=1) * onehot, axis=-1)) - 1
    slots = expert_ids * CAP + ranks
    targets = (jnp.arange(devices, dtype=jnp.int32)[:, None] * (EXPERTS * CAP) + slots).reshape(-1)

    def to_experts(values):
        store = jnp.zeros((devices * EXPERTS * CAP, D), jnp.bfloat16).at[targets].set(values.reshape(-1, D))
        store = store.reshape(devices, EXPERTS, CAP, D).transpose(1, 0, 2, 3)
        return store.reshape(EXPERTS, N_DP, N_EXPERT * CAP, D)

    def from_experts(values):
        store = values.reshape(EXPERTS, devices, CAP, D).transpose(1, 0, 2, 3).reshape(devices * EXPERTS * CAP, D)
        return store[targets].reshape(devices, TOK_DEV, D)

    def expert_work(args):
        inputs, grads, up_mat, down_mat = args
        inputs_f = inputs.astype(jnp.float32)
        grads_f = grads.astype(jnp.float32)
        pre_act = jnp.einsum('rsd,df->rsf', inputs_f, up_mat.astype(jnp.float32))
        hidden = gelu_tanh(pre_act).astype(jnp.bfloat16)
        hidden_f = hidden.astype(jnp.float32)
        result = jnp.einsum('rsf,fd->rsd', hidden_f, down_mat.astype(jnp.float32)).astype(jnp.bfloat16)
        d_hidden = jnp.einsum('rsd,fd->rsf', grads_f, down_mat.astype(jnp.float32))
        d_pre = gelu_back(pre_act, d_hidden).astype(jnp.bfloat16)
        d_pre_f = d_pre.astype(jnp.float32)
        part_up = lax.optimization_barrier(jnp.einsum('rsd,rsf->rdf', inputs_f, d_pre_f).astype(jnp.bfloat16))
        part_down = lax.optimization_barrier(jnp.einsum('rsf,rsd->rfd', hidden_f, grads_f).astype(jnp.bfloat16))
        d_inner = jnp.einsum('rsf,df->rsd', d_pre_f, up_mat.astype(jnp.float32)).astype(jnp.bfloat16)
        return (result, d_inner, lax.optimization_barrier(jnp.sum(part_up.astype(jnp.float32), axis=0)), lax.optimization_barrier(jnp.sum(part_down.astype(jnp.float32), axis=0)))
    results, d_inners, grad_up, grad_down = lax.map(expert_work, (to_experts(inner), to_experts(cot_dev), w_up, w_down))
    expert_out = from_experts(results)
    d_inner = from_experts(d_inners)
    out = (resid.astype(jnp.float32) + expert_out.astype(jnp.float32)).astype(jnp.bfloat16)

    def backward(carry, args):
        x_part, label_part, resid_part, d_inner_part, cot_part = args
        x_f = x_part.astype(jnp.float32)
        normed, norm_x_back = jax.vjp(rms_norm, x_f)
        packed = jnp.dot(normed, w_qkv, preferred_element_type=jnp.float32).astype(jnp.bfloat16)
        mixed, core_back = jax.vjp(lambda value: attention_core(value, label_part), packed)
        resid_unused, norm_h_back = jax.vjp(rms_norm, resid_part.astype(jnp.float32))
        d_resid = (cot_part.astype(jnp.float32) + norm_h_back(d_inner_part)[0]).astype(jnp.bfloat16)
        grad_o_part = row_contract(d_resid, mixed)
        d_mixed = jnp.dot(d_resid, w_o, preferred_element_type=jnp.float32).astype(jnp.bfloat16)
        d_packed = core_back(d_mixed)[0]
        grad_qkv_part = row_contract(normed, d_packed)
        d_normed = col_contract(d_packed, w_qkv).astype(jnp.bfloat16)
        grad_part = (d_resid.astype(jnp.float32) + norm_x_back(d_normed)[0]).astype(jnp.bfloat16)
        return ((carry[0] + grad_qkv_part, carry[1] + grad_o_part), grad_part)
    start = (jnp.zeros((D, 3 * HEADS * HD), jnp.float32), jnp.zeros((D, HEADS * HD), jnp.float32))
    totals, grad_input = lax.scan(backward, start, (x_dev, label_dev, resid, d_inner, cot_dev))
    return (out.reshape(TOKENS, D), grad_input.reshape(TOKENS, D), totals[0], totals[1], grad_up, grad_down)
```

```python
import jax
import jax.numpy as jnp
from jax import lax
from jax.sharding import PartitionSpec as P

HD = 64


EPSILON = 1e-06


def rms_norm(values):
    scale = lax.rsqrt(jnp.mean(values * values, axis=-1, keepdims=True) + EPSILON)
    return (values * scale).astype(jnp.bfloat16)


def gelu_tanh(values):
    return jax.nn.gelu(values, approximate=True)


def gelu_back(pre_act, cotangent):
    return jax.vjp(gelu_tanh, pre_act)[1](cotangent)[0]


def row_contract(left, right):
    return lax.dot_general(
        left, right, (((0,), (0,)), ((), ())), preferred_element_type=jnp.float32
    )


def col_contract(left, right):
    return lax.dot_general(
        left, right, (((1,), (1,)), ((), ())), preferred_element_type=jnp.float32
    )


def attention_core(packed, labels_row):
    rows = packed.shape[0]
    blocks = rows // 128
    width = packed.shape[1] // 3
    heads = width // HD
    parts = packed.reshape(blocks, 128, 3, heads, HD)
    query = parts[:, :, 0]
    keys = parts[:, :, 1]
    values = parts[:, :, 2]
    scores = jnp.einsum(
        "bqhc,bkhc->bhqk", query, keys, preferred_element_type=jnp.float32
    ) * HD ** (-0.5)
    labels = labels_row.reshape(blocks, 128)
    same = (labels[:, :, None] == labels[:, None, :])[:, None]
    weights = jnp.where(same, jnp.exp(scores), 0.0)
    probs = (weights / jnp.sum(weights, axis=-1, keepdims=True)).astype(jnp.bfloat16)
    mixed = jnp.einsum("bhqk,bkhc->bqhc", probs, values, preferred_element_type=jnp.float32)
    return mixed.astype(jnp.bfloat16).reshape(rows, width)


def stage_perm(count, bit):
    return [(i, i ^ bit) for i in range(count)]


def halve(values, axis_name, count, axis, bit):
    own = (lax.axis_index(axis_name) // bit) % 2
    keep = lax.dynamic_index_in_dim(values, own, axis, keepdims=False)
    give = lax.dynamic_index_in_dim(values, 1 - own, axis, keepdims=False).astype(jnp.bfloat16)
    came = lax.ppermute(give, axis_name, stage_perm(count, bit))
    return keep + came.astype(jnp.float32)


def scatter_sum(term):
    groups, shards = lax.axis_size("dp"), lax.axis_size("expert")
    rows, cols = term.shape
    own_rows = rows // (groups * shards)
    left = shards
    value = term.reshape(groups * shards * own_rows, cols)
    lead = groups
    bit = 1
    while bit < shards:
        left //= 2
        value = halve(value.reshape(lead, left, 2, own_rows, cols), "expert", shards, 2, bit)
        bit *= 2
    left = groups
    bit = 1
    while bit < groups:
        left //= 2
        value = halve(value.reshape(left, 2, own_rows, cols), "dp", groups, 1, bit)
        bit *= 2
    return value.reshape(own_rows, cols)


def ring_pairs(groups, step):
    half = groups // 2
    return [(i, ((i // 2 + step) % half) * 2 + i % 2) for i in range(groups)]


def ring_gather(shard, pairs, count):
    slots = [shard]
    for _ in range(count - 1):
        slots.append(lax.ppermute(slots[-1], "dp", pairs))
    return slots


def ring_reduce(slots, pairs):
    count = len(slots)
    total = slots[1 % count]
    for step in range(count - 1):
        came = lax.ppermute(total.astype(jnp.bfloat16), "dp", pairs)
        total = came.astype(jnp.float32) + slots[(step + 2) % count]
    return total


def on_device(layer_in, body_of, expert_of, w_qkv, w_o, w_up, w_down, d_out):
    tok_rows = layer_in.shape[0]
    width = layer_in.shape[1]
    shards = lax.axis_size("expert")
    groups = lax.axis_size("dp")
    half = groups // 2
    local_experts = w_up.shape[0]
    all_experts = local_experts * shards
    capacity = 3 * tok_rows // (2 * all_experts)
    received = shards * capacity
    partner = stage_perm(groups, 1)
    forth, back = ring_pairs(groups, 1), ring_pairs(groups, -1)

    full_up = jnp.concatenate(ring_gather(w_up, forth, half), axis=2)
    full_down = jnp.concatenate(ring_gather(w_down, forth, half), axis=1)

    ids = expert_of[:, 0]
    at = jnp.arange(tok_rows, dtype=jnp.int32)
    earlier = (ids[:, None] == ids[None, :]) & (at[None, :] < at[:, None])
    ranks = jnp.sum(earlier.astype(jnp.int32), axis=1)
    slots = ids * capacity + ranks
    places = jnp.arange(all_experts * capacity, dtype=jnp.int32)
    spread = (places[:, None] == slots[None, :]).astype(jnp.bfloat16)

    def to_experts(values):
        store = jnp.dot(spread, values, preferred_element_type=jnp.float32).astype(jnp.bfloat16)
        store = store.reshape(shards, local_experts, capacity, width)
        sent = lax.all_to_all(store, "expert", split_axis=0, concat_axis=2, tiled=True)
        own = sent.reshape(local_experts, received, width)
        return jnp.concatenate([own, lax.ppermute(own, "dp", partner)], axis=1)

    def to_tokens(values):
        other = lax.ppermute(values[:, received:].astype(jnp.bfloat16), "dp", partner)
        total = (values[:, :received] + other.astype(jnp.float32)).astype(jnp.bfloat16)
        total = total.reshape(local_experts, shards, capacity, width)
        returned = lax.all_to_all(total, "expert", split_axis=1, concat_axis=0, tiled=True)
        returned = returned.reshape(all_experts * capacity, width)
        return row_contract(spread, returned)

    grads_in = to_experts(d_out)
    layer_f = layer_in.astype(jnp.float32)
    normed, norm_x_back = jax.vjp(rms_norm, layer_f)
    packed = jnp.dot(normed, w_qkv, preferred_element_type=jnp.float32).astype(jnp.bfloat16)
    mixed, core_back = jax.vjp(lambda value: attention_core(value, body_of), packed)
    resid = (layer_f + col_contract(mixed, w_o)).astype(jnp.bfloat16)
    inner, norm_h_back = jax.vjp(rms_norm, resid.astype(jnp.float32))
    inputs = to_experts(inner)
    d_hidden = jnp.einsum("esd,efd->esf", grads_in, full_down, preferred_element_type=jnp.float32)
    pre_act = jnp.einsum("esd,edf->esf", inputs, full_up, preferred_element_type=jnp.float32)
    hidden = gelu_tanh(pre_act).astype(jnp.bfloat16)
    d_pre = gelu_back(pre_act, d_hidden).astype(jnp.bfloat16)
    d_inputs = jnp.einsum("esf,edf->esd", d_pre, full_up, preferred_element_type=jnp.float32)
    d_inner = to_tokens(d_inputs).astype(jnp.bfloat16)
    part_up = jnp.einsum("esd,esf->edf", inputs, d_pre, preferred_element_type=jnp.float32)
    part_down = jnp.einsum("esf,esd->efd", hidden, grads_in, preferred_element_type=jnp.float32)
    grad_up = ring_reduce(jnp.split(part_up, half, axis=2), forth)
    grad_down = ring_reduce(jnp.split(part_down, half, axis=1), forth)
    result = jnp.einsum("esf,efd->esd", hidden, full_down, preferred_element_type=jnp.float32)
    expert_out = to_tokens(result)
    out = (resid.astype(jnp.float32) + expert_out).astype(jnp.bfloat16)
    d_resid = (d_out.astype(jnp.float32) + norm_h_back(d_inner)[0]).astype(jnp.bfloat16)
    grad_o = scatter_sum(row_contract(d_resid, mixed))
    d_mixed = jnp.dot(d_resid, w_o, preferred_element_type=jnp.float32).astype(jnp.bfloat16)
    d_packed = core_back(d_mixed)[0]
    grad_qkv = scatter_sum(row_contract(normed, d_packed))
    d_normed = col_contract(d_packed, w_qkv).astype(jnp.bfloat16)
    grad_input = (d_resid.astype(jnp.float32) + norm_x_back(d_normed)[0]).astype(jnp.bfloat16)
    return (out, grad_input, grad_qkv, grad_o, grad_up, grad_down)


def solution(mesh):
    in_specs = (
        P(("dp", "expert"), None),
        P(("dp", "expert")),
        P(("dp", "expert"), None),
        P(),
        P(),
        P("expert", None, "dp"),
        P("expert", "dp", None),
        P(("dp", "expert"), None),
    )
    out_specs = (
        P(("dp", "expert"), None),
        P(("dp", "expert"), None),
        P(("dp", "expert"), None),
        P(("dp", "expert"), None),
        P("expert", None, "dp"),
        P("expert", "dp", None),
    )
    return jax.shard_map(
        on_device, mesh=mesh, in_specs=in_specs, out_specs=out_specs, check_vma=False
    )
```

```python
import jax
import jax.numpy as jnp
from jax import lax
from jax.experimental import pallas as pl
from jax.experimental.pallas import tpu as pltpu
from jax.sharding import PartitionSpec as P

HD = 64


EPSILON = 1e-06


def rms_norm(values):
    scale = lax.rsqrt(jnp.mean(values * values, axis=-1, keepdims=True) + EPSILON)
    return (values * scale).astype(jnp.bfloat16)


def gelu_tanh(values):
    return jax.nn.gelu(values, approximate=True)


def gelu_back(pre_act, cotangent):
    return jax.vjp(gelu_tanh, pre_act)[1](cotangent)[0]


def row_contract(left, right):
    return lax.dot_general(
        left, right, (((0,), (0,)), ((), ())), preferred_element_type=jnp.float32
    )


def col_contract(left, right):
    return lax.dot_general(
        left, right, (((1,), (1,)), ((), ())), preferred_element_type=jnp.float32
    )


def softmax_parts(packed_ref, rows, pair, side, width, same, first):
    query = packed_ref[rows, pl.ds(pair * 128, 128)]
    keys = packed_ref[rows, pl.ds(width + pair * 128, 128)]
    mine = first if side == 0 else jnp.logical_not(first)
    query = jnp.where(mine, query, jnp.zeros_like(query))
    scores = col_contract(query, keys) * HD ** (-0.5)
    weights = jnp.where(same, jnp.exp(scores), 0.0)
    return weights / jnp.sum(weights, axis=-1, keepdims=True)


def first_half():
    return lax.broadcasted_iota(jnp.int32, (128, 128), 1) < HD


def front_kernel(x_ref, col_ref, row_ref, qkv_ref, wo_ref, normed_ref, packed_ref, mixed_ref, resid_ref, inner_ref):
    width = mixed_ref.shape[1]
    first = first_half()
    normed_ref[...] = rms_norm(x_ref[...].astype(jnp.float32))
    packed_ref[...] = jnp.dot(
        normed_ref[...], qkv_ref[...], preferred_element_type=jnp.float32
    ).astype(jnp.bfloat16)
    for block in range(x_ref.shape[0] // 128):
        rows = pl.ds(block * 128, 128)
        same = col_ref[rows, :] == row_ref[:, rows]
        for pair in range(width // 128):
            values = packed_ref[rows, pl.ds(2 * width + pair * 128, 128)]
            heads = []
            for side in range(2):
                probs = softmax_parts(packed_ref, rows, pair, side, width, same, first)
                heads.append(
                    jnp.dot(probs.astype(jnp.bfloat16), values, preferred_element_type=jnp.float32)
                )
            mixed_ref[rows, pl.ds(pair * 128, 128)] = jnp.where(first, heads[0], heads[1]).astype(
                jnp.bfloat16
            )
    resid = (x_ref[...].astype(jnp.float32) + col_contract(mixed_ref[...], wo_ref[...])).astype(
        jnp.bfloat16
    )
    resid_ref[...] = resid
    inner_ref[...] = rms_norm(resid.astype(jnp.float32))


def back_kernel(grad_ref, col_ref, row_ref, wo_ref, packed_ref, out_ref, mixed_grad_ref):
    width = wo_ref.shape[1]
    first = first_half()
    mixed_grad_ref[...] = jnp.dot(
        grad_ref[...], wo_ref[...], preferred_element_type=jnp.float32
    ).astype(jnp.bfloat16)
    for block in range(grad_ref.shape[0] // 128):
        rows = pl.ds(block * 128, 128)
        same = col_ref[rows, :] == row_ref[:, rows]
        for pair in range(width // 128):
            query = packed_ref[rows, pl.ds(pair * 128, 128)]
            keys = packed_ref[rows, pl.ds(width + pair * 128, 128)]
            values = packed_ref[rows, pl.ds(2 * width + pair * 128, 128)]
            d_mixed = mixed_grad_ref[rows, pl.ds(pair * 128, 128)]
            parts = []
            for side in range(2):
                mine = first if side == 0 else jnp.logical_not(first)
                probs = softmax_parts(packed_ref, rows, pair, side, width, same, first)
                d_values = row_contract(probs.astype(jnp.bfloat16), d_mixed)
                d_probs = col_contract(jnp.where(mine, d_mixed, jnp.zeros_like(d_mixed)), values)
                d_probs = d_probs.astype(jnp.bfloat16).astype(jnp.float32)
                inside = jnp.sum(d_probs * probs, axis=-1, keepdims=True)
                d_scores = (probs * (d_probs - inside) * HD ** (-0.5)).astype(jnp.bfloat16)
                d_query = jnp.dot(d_scores, keys, preferred_element_type=jnp.float32)
                d_keys = row_contract(d_scores, query)
                parts.append((d_query, d_keys, d_values))
            for at, (left, right) in enumerate(zip(*parts)):
                out_ref[rows, pl.ds(at * width + pair * 128, 128)] = jnp.where(
                    first, left, right
                ).astype(jnp.bfloat16)


def front(x, col, row, w_qkv, w_o):
    rows, width = x.shape[0], w_o.shape[1]
    shape = lambda cols: jax.ShapeDtypeStruct((rows, cols), jnp.bfloat16)
    return pl.pallas_call(
        front_kernel,
        out_shape=[shape(x.shape[1]), shape(3 * width), shape(width), shape(x.shape[1]), shape(x.shape[1])],
        compiler_params=pltpu.CompilerParams(vmem_limit_bytes=40 * 1024 * 1024),
        cost_estimate=pl.CostEstimate(flops=6 * 10**9, bytes_accessed=7 * 10**6, transcendentals=0),
        name="front",
    )(x, col, row, w_qkv, w_o)


def attention_back(d_resid, col, row, w_o, packed):
    return pl.pallas_call(
        back_kernel,
        out_shape=jax.ShapeDtypeStruct(packed.shape, jnp.bfloat16),
        scratch_shapes=[pltpu.VMEM((packed.shape[0], w_o.shape[1]), jnp.bfloat16)],
        compiler_params=pltpu.CompilerParams(vmem_limit_bytes=40 * 1024 * 1024),
        cost_estimate=pl.CostEstimate(flops=6 * 10**9, bytes_accessed=7 * 10**6, transcendentals=0),
        name="attention_back",
    )(d_resid, col, row, w_o, packed)


def norm_back(values, cotangent):
    scale = lax.rsqrt(jnp.mean(values * values, axis=-1, keepdims=True) + EPSILON)
    along = jnp.mean(values * cotangent, axis=-1, keepdims=True)
    return scale * (cotangent - values * (scale * scale * along))


def stage_perm(count, bit):
    return [(i, i ^ bit) for i in range(count)]


def halve(values, axis_name, count, axis, bit):
    own = (lax.axis_index(axis_name) // bit) % 2
    keep = lax.dynamic_index_in_dim(values, own, axis, keepdims=True)
    give = lax.dynamic_index_in_dim(values, 1 - own, axis, keepdims=True).astype(jnp.bfloat16)
    came = lax.ppermute(give, axis_name, stage_perm(count, bit))
    return keep + came.astype(jnp.float32)


def scatter_sum(term, late_y):
    groups, shards = lax.axis_size("dp"), lax.axis_size("expert")
    rows, cols = term.shape
    bits = []
    for name, count in (("dp", groups), ("expert", shards)):
        bit = count // 2
        while bit:
            bits.append((name, count, bit))
            bit //= 2
    value = term.reshape((2,) * len(bits) + (rows // (groups * shards), cols))
    expert_bits = [b for b in reversed(bits) if b[0] == "expert"]
    group_bits = [b for b in reversed(bits) if b[0] == "dp"]
    if late_y:
        order = expert_bits[:1] + group_bits[:1] + expert_bits[1:] + group_bits[1:]
    else:
        order = expert_bits + group_bits
    for one in order:
        value = halve(value, one[0], one[1], bits.index(one), one[2])
    return value.reshape(rows // (groups * shards), cols)


def ring_pairs(groups, step):
    half = groups // 2
    return [(i, ((i // 2 + step) % half) * 2 + i % 2) for i in range(groups)]


def gather_step(slots, pairs):
    return slots + [lax.ppermute(slots[-1], "dp", pairs)]


def reduce_step(total, slots, step, pairs):
    came = lax.ppermute(total.astype(jnp.bfloat16), "dp", pairs)
    return came.astype(jnp.float32) + slots[(step + 2) % len(slots)]


def on_device(layer_in, body_of, expert_of, w_qkv, w_o, w_up, w_down, d_out):
    tok_rows = layer_in.shape[0]
    width = layer_in.shape[1]
    shards = lax.axis_size("expert")
    groups = lax.axis_size("dp")
    half = groups // 2
    local_experts = w_up.shape[0]
    all_experts = local_experts * shards
    capacity = 3 * tok_rows // (2 * all_experts)
    received = shards * capacity
    partner = stage_perm(groups, 1)
    forth, back = ring_pairs(groups, 1), ring_pairs(groups, -1)

    ups, downs = gather_step([w_up], forth), gather_step([w_down], forth)

    ids = expert_of[:, 0]
    at = jnp.arange(tok_rows, dtype=jnp.int32)
    earlier = (ids[:, None] == ids[None, :]) & (at[None, :] < at[:, None])
    ranks = jnp.sum(earlier.astype(jnp.int32), axis=1)
    slots = ids * capacity + ranks
    places = jnp.arange(all_experts * capacity, dtype=jnp.int32)
    spread = (places[:, None] == slots[None, :]).astype(jnp.bfloat16)

    def to_slots(values):
        store = jnp.dot(spread, values, preferred_element_type=jnp.float32).astype(jnp.bfloat16)
        return store.reshape(shards, local_experts, capacity, width)

    def exchange(store):
        sent = lax.all_to_all(store, "expert", split_axis=0, concat_axis=2, tiled=True)
        return sent.reshape(local_experts, received, width)

    def with_partner(own):
        return jnp.concatenate([own, lax.ppermute(own, "dp", partner)], axis=1)

    def to_tokens(values):
        other = lax.ppermute(values[:, received:].astype(jnp.bfloat16), "dp", partner)
        total = (values[:, :received] + other.astype(jnp.float32)).astype(jnp.bfloat16)
        total = total.reshape(local_experts, shards, capacity, width)
        returned = lax.all_to_all(total, "expert", split_axis=1, concat_axis=0, tiled=True)
        returned = returned.reshape(all_experts * capacity, width)
        return row_contract(spread, returned)

    col, row = body_of[:, None], body_of[None, :]
    store, layer_in = lax.optimization_barrier((to_slots(d_out), layer_in))
    own_grads = exchange(store)
    normed, packed, mixed, resid, inner = front(layer_in, col, row, w_qkv, w_o)
    store, own_grads, ups, downs = lax.optimization_barrier((to_slots(inner), own_grads, ups, downs))
    ups, downs = gather_step(ups, forth), gather_step(downs, forth)
    grads_in = with_partner(own_grads)
    own_inputs, ups, downs = lax.optimization_barrier((exchange(store), ups, downs))
    inputs = with_partner(own_inputs)
    while len(ups) < half:
        ups, downs = gather_step(ups, forth), gather_step(downs, forth)
    full_up = jnp.concatenate(ups, axis=2)
    full_down = jnp.concatenate(downs, axis=1)
    d_hidden = jnp.einsum("esd,efd->esf", grads_in, full_down, preferred_element_type=jnp.float32)
    pre_act = jnp.einsum("esd,edf->esf", inputs, full_up, preferred_element_type=jnp.float32)
    hidden = gelu_tanh(pre_act).astype(jnp.bfloat16)
    d_pre = gelu_back(pre_act, d_hidden).astype(jnp.bfloat16)
    d_inputs = jnp.einsum("esf,edf->esd", d_pre, full_up, preferred_element_type=jnp.float32)
    d_inner = to_tokens(d_inputs).astype(jnp.bfloat16)
    part_down = jnp.einsum("esf,esd->efd", hidden, grads_in, preferred_element_type=jnp.float32)
    part_up = jnp.einsum("esd,esf->edf", inputs, d_pre, preferred_element_type=jnp.float32)
    slots_up = jnp.split(part_up, half, axis=2)
    slots_down = jnp.split(part_down, half, axis=1)
    grad_up = reduce_step(slots_up[1], slots_up, 0, forth)
    grad_down = reduce_step(slots_down[1], slots_down, 0, forth)
    result = jnp.einsum("esf,efd->esd", hidden, full_down, preferred_element_type=jnp.float32)
    expert_out = to_tokens(result)
    out = (resid.astype(jnp.float32) + expert_out).astype(jnp.bfloat16)
    d_inner, grad_up, grad_down = lax.optimization_barrier((d_inner, grad_up, grad_down))
    grad_up = reduce_step(grad_up, slots_up, 1, forth)
    grad_down = reduce_step(grad_down, slots_down, 1, forth)
    resid_grad = norm_back(resid.astype(jnp.float32), d_inner.astype(jnp.float32))
    d_resid = (d_out.astype(jnp.float32) + resid_grad).astype(jnp.bfloat16)
    grad_o = scatter_sum(row_contract(d_resid, mixed), True)
    d_packed = attention_back(d_resid, col, row, w_o, packed)
    d_packed, grad_up, grad_down = lax.optimization_barrier((d_packed, grad_up, grad_down))
    for step in range(2, half - 1):
        grad_up = reduce_step(grad_up, slots_up, step, forth)
        grad_down = reduce_step(grad_down, slots_down, step, forth)
    split = d_packed.shape[1] // 2
    grad_qkv = jnp.concatenate(
        [
            scatter_sum(row_contract(normed, d_packed[:, :split]), False),
            scatter_sum(row_contract(normed, d_packed[:, split:]), True),
        ],
        axis=1,
    )
    d_normed = col_contract(d_packed, w_qkv).astype(jnp.bfloat16)
    input_grad = norm_back(layer_in.astype(jnp.float32), d_normed.astype(jnp.float32))
    grad_input = (d_resid.astype(jnp.float32) + input_grad).astype(jnp.bfloat16)
    return (out, grad_input, grad_qkv, grad_o, grad_up, grad_down)


def solution(mesh):
    in_specs = (
        P(("dp", "expert"), None),
        P(("dp", "expert")),
        P(("dp", "expert"), None),
        P(),
        P(),
        P("expert", None, "dp"),
        P("expert", "dp", None),
        P(("dp", "expert"), None),
    )
    out_specs = (
        P(("dp", "expert"), None),
        P(("dp", "expert"), None),
        P(("dp", "expert"), None),
        P(("dp", "expert"), None),
        P("expert", None, "dp"),
        P("expert", "dp", None),
    )
    return jax.shard_map(
        on_device, mesh=mesh, in_specs=in_specs, out_specs=out_specs, check_vma=False
    )
```

```python
import jax
import jax.numpy as jnp
from jax import lax
from jax.experimental import pallas as pl
from jax.experimental.pallas import tpu as pltpu
from jax.sharding import PartitionSpec as P

HD = 64


EPSILON = 1e-06


def rms_norm(values):
    scale = lax.rsqrt(jnp.mean(values * values, axis=-1, keepdims=True) + EPSILON)
    return (values * scale).astype(jnp.bfloat16)


def gelu_tanh(values):
    return jax.nn.gelu(values, approximate=True)


def gelu_back(pre_act, cotangent):
    return jax.vjp(gelu_tanh, pre_act)[1](cotangent)[0]


def row_contract(left, right):
    return lax.dot_general(
        left, right, (((0,), (0,)), ((), ())), preferred_element_type=jnp.float32
    )


def col_contract(left, right):
    return lax.dot_general(
        left, right, (((1,), (1,)), ((), ())), preferred_element_type=jnp.float32
    )


def softmax_parts(packed_ref, rows, pair, side, width, same, first):
    query = packed_ref[rows, pl.ds(pair * 128, 128)]
    keys = packed_ref[rows, pl.ds(width + pair * 128, 128)]
    mine = first if side == 0 else jnp.logical_not(first)
    query = jnp.where(mine, query, jnp.zeros_like(query))
    scores = col_contract(query, keys) * HD ** (-0.5)
    weights = jnp.where(same, jnp.exp(scores), 0.0)
    return weights / jnp.sum(weights, axis=-1, keepdims=True)


def first_half():
    return lax.broadcasted_iota(jnp.int32, (128, 128), 1) < HD


def front_kernel(x_ref, col_ref, row_ref, qkv_ref, wo_ref, normed_ref, packed_ref, mixed_ref, resid_ref, inner_ref):
    width = mixed_ref.shape[1]
    first = first_half()
    normed_ref[...] = rms_norm(x_ref[...].astype(jnp.float32))
    packed_ref[...] = jnp.dot(
        normed_ref[...], qkv_ref[...], preferred_element_type=jnp.float32
    ).astype(jnp.bfloat16)
    for block in range(x_ref.shape[0] // 128):
        rows = pl.ds(block * 128, 128)
        same = col_ref[rows, :] == row_ref[:, rows]
        for pair in range(width // 128):
            values = packed_ref[rows, pl.ds(2 * width + pair * 128, 128)]
            heads = []
            for side in range(2):
                probs = softmax_parts(packed_ref, rows, pair, side, width, same, first)
                heads.append(
                    jnp.dot(probs.astype(jnp.bfloat16), values, preferred_element_type=jnp.float32)
                )
            mixed_ref[rows, pl.ds(pair * 128, 128)] = jnp.where(first, heads[0], heads[1]).astype(
                jnp.bfloat16
            )
    resid = (x_ref[...].astype(jnp.float32) + col_contract(mixed_ref[...], wo_ref[...])).astype(
        jnp.bfloat16
    )
    resid_ref[...] = resid
    inner_ref[...] = rms_norm(resid.astype(jnp.float32))


def back_kernel(grad_ref, col_ref, row_ref, wo_ref, packed_ref, normed_ref, mixed_ref, out_ref, left_ref, right_ref, mixed_grad_ref):
    width = wo_ref.shape[1]
    first = first_half()
    mixed_grad_ref[...] = jnp.dot(
        grad_ref[...], wo_ref[...], preferred_element_type=jnp.float32
    ).astype(jnp.bfloat16)
    for block in range(grad_ref.shape[0] // 128):
        rows = pl.ds(block * 128, 128)
        same = col_ref[rows, :] == row_ref[:, rows]
        for pair in range(width // 128):
            query = packed_ref[rows, pl.ds(pair * 128, 128)]
            keys = packed_ref[rows, pl.ds(width + pair * 128, 128)]
            values = packed_ref[rows, pl.ds(2 * width + pair * 128, 128)]
            d_mixed = mixed_grad_ref[rows, pl.ds(pair * 128, 128)]
            parts = []
            for side in range(2):
                mine = first if side == 0 else jnp.logical_not(first)
                probs = softmax_parts(packed_ref, rows, pair, side, width, same, first)
                d_values = row_contract(probs.astype(jnp.bfloat16), d_mixed)
                d_probs = col_contract(jnp.where(mine, d_mixed, jnp.zeros_like(d_mixed)), values)
                d_probs = d_probs.astype(jnp.bfloat16).astype(jnp.float32)
                inside = jnp.sum(d_probs * probs, axis=-1, keepdims=True)
                d_scores = (probs * (d_probs - inside) * HD ** (-0.5)).astype(jnp.bfloat16)
                d_query = jnp.dot(d_scores, keys, preferred_element_type=jnp.float32)
                d_keys = row_contract(d_scores, query)
                parts.append((d_query, d_keys, d_values))
            for at, (left, right) in enumerate(zip(*parts)):
                out_ref[rows, pl.ds(at * width + pair * 128, 128)] = jnp.where(
                    first, left, right
                ).astype(jnp.bfloat16)
    add_terms(grad_ref, normed_ref, mixed_ref, out_ref, left_ref, right_ref)


def add_terms(grad_ref, normed_ref, mixed_ref, out_ref, left_ref, right_ref):
    width = mixed_ref.shape[1]
    left_ref[...] = row_contract(normed_ref[...], out_ref[:, : 2 * width])
    right_ref[:, :width] = row_contract(normed_ref[...], out_ref[:, 2 * width :])
    right_ref[:, width:] = row_contract(grad_ref[...], mixed_ref[...])


def front(x, col, row, w_qkv, w_o):
    rows, width = x.shape[0], w_o.shape[1]
    shape = lambda cols: jax.ShapeDtypeStruct((rows, cols), jnp.bfloat16)
    return pl.pallas_call(
        front_kernel,
        out_shape=[shape(x.shape[1]), shape(3 * width), shape(width), shape(x.shape[1]), shape(x.shape[1])],
        compiler_params=pltpu.CompilerParams(vmem_limit_bytes=40 * 1024 * 1024),
        cost_estimate=pl.CostEstimate(flops=6 * 10**9, bytes_accessed=7 * 10**6, transcendentals=0),
        name="front",
    )(x, col, row, w_qkv, w_o)


def attention_back(d_resid, col, row, w_o, packed, normed, mixed):
    term = jax.ShapeDtypeStruct((normed.shape[1], 2 * mixed.shape[1]), jnp.float32)
    return pl.pallas_call(
        back_kernel,
        out_shape=[jax.ShapeDtypeStruct(packed.shape, jnp.bfloat16), term, term],
        scratch_shapes=[pltpu.VMEM((packed.shape[0], w_o.shape[1]), jnp.bfloat16)],
        compiler_params=pltpu.CompilerParams(vmem_limit_bytes=48 * 1024 * 1024),
        cost_estimate=pl.CostEstimate(flops=6 * 10**9, bytes_accessed=16 * 10**6, transcendentals=0),
        name="attention_back",
    )(d_resid, col, row, w_o, packed, normed, mixed)


def norm_back(values, cotangent):
    scale = lax.rsqrt(jnp.mean(values * values, axis=-1, keepdims=True) + EPSILON)
    along = jnp.mean(values * cotangent, axis=-1, keepdims=True)
    return scale * (cotangent - values * (scale * scale * along))


def stage_perm(count, bit):
    return [(i, i ^ bit) for i in range(count)]


def halve(values, axis_name, count, axis, bit):
    own = (lax.axis_index(axis_name) // bit) % 2
    keep = lax.dynamic_index_in_dim(values, own, axis, keepdims=True)
    give = lax.dynamic_index_in_dim(values, 1 - own, axis, keepdims=True).astype(jnp.bfloat16)
    came = lax.ppermute(give, axis_name, stage_perm(count, bit))
    return keep + came.astype(jnp.float32)


def halving_steps(late_y):
    bits = []
    for name in ("dp", "expert"):
        count = lax.axis_size(name)
        bit = count // 2
        while bit:
            bits.append((name, count, len(bits), bit))
            bit //= 2
    expert_bits = [b for b in reversed(bits) if b[0] == "expert"]
    group_bits = [b for b in reversed(bits) if b[0] == "dp"]
    if late_y:
        return expert_bits[:1] + group_bits[:1] + expert_bits[1:] + group_bits[1:]
    return expert_bits + group_bits


def ring_pairs(groups, step):
    half = groups // 2
    return [(i, ((i // 2 + step) % half) * 2 + i % 2) for i in range(groups)]


def gather_step(slots, pairs):
    return slots + [lax.ppermute(slots[-1], "dp", pairs)]


def turned(slots):
    return slots[:1] + slots[:0:-1]


def reduce_step(total, slots, step, pairs):
    came = lax.ppermute(total.astype(jnp.bfloat16), "dp", pairs)
    return came.astype(jnp.float32) + slots[(step + 2) % len(slots)]


def on_device(layer_in, body_of, expert_of, w_qkv, w_o, w_up, w_down, d_out):
    tok_rows = layer_in.shape[0]
    width = layer_in.shape[1]
    shards = lax.axis_size("expert")
    groups = lax.axis_size("dp")
    half = groups // 2
    local_experts = w_up.shape[0]
    all_experts = local_experts * shards
    capacity = 3 * tok_rows // (2 * all_experts)
    received = shards * capacity
    partner = stage_perm(groups, 1)
    forth, back = ring_pairs(groups, 1), ring_pairs(groups, -1)

    ups, downs = gather_step([w_up], forth), gather_step([w_down], back)

    ids = expert_of[:, 0]
    at = jnp.arange(tok_rows, dtype=jnp.int32)
    earlier = (ids[:, None] == ids[None, :]) & (at[None, :] < at[:, None])
    ranks = jnp.sum(earlier.astype(jnp.int32), axis=1)
    slots = ids * capacity + ranks
    places = jnp.arange(all_experts * capacity, dtype=jnp.int32)
    spread = (places[:, None] == slots[None, :]).astype(jnp.bfloat16)

    def to_slots(values):
        store = jnp.dot(spread, values, preferred_element_type=jnp.float32).astype(jnp.bfloat16)
        return store.reshape(shards, local_experts, capacity, width)

    def exchange(store):
        sent = lax.all_to_all(store, "expert", split_axis=0, concat_axis=2, tiled=True)
        return sent.reshape(local_experts, received, width)

    def with_partner(own):
        return jnp.concatenate([own, lax.ppermute(own, "dp", partner)], axis=1)

    def to_tokens(values):
        other = lax.ppermute(values[:, received:].astype(jnp.bfloat16), "dp", partner)
        total = (values[:, :received] + other.astype(jnp.float32)).astype(jnp.bfloat16)
        total = total.reshape(local_experts, shards, capacity, width)
        returned = lax.all_to_all(total, "expert", split_axis=1, concat_axis=0, tiled=True)
        returned = returned.reshape(all_experts * capacity, width)
        return row_contract(spread, returned)

    col, row = body_of[:, None], body_of[None, :]
    store, layer_in = lax.optimization_barrier((to_slots(d_out), layer_in))
    own_grads = exchange(store)
    normed, packed, mixed, resid, inner = front(layer_in, col, row, w_qkv, w_o)
    store, own_grads, ups, downs = lax.optimization_barrier((to_slots(inner), own_grads, ups, downs))
    ups, downs = gather_step(ups, forth), gather_step(downs, back)
    grads_in = with_partner(own_grads)
    own_inputs, ups, downs = lax.optimization_barrier((exchange(store), ups, downs))
    inputs = with_partner(own_inputs)
    while len(ups) < half:
        ups, downs = gather_step(ups, forth), gather_step(downs, back)
    full_up = jnp.concatenate(ups, axis=2)
    full_down = jnp.concatenate(turned(downs), axis=1)
    d_hidden = jnp.einsum("esd,efd->esf", grads_in, full_down, preferred_element_type=jnp.float32)
    pre_act = jnp.einsum("esd,edf->esf", inputs, full_up, preferred_element_type=jnp.float32)
    hidden = gelu_tanh(pre_act).astype(jnp.bfloat16)
    d_pre = gelu_back(pre_act, d_hidden).astype(jnp.bfloat16)
    d_inputs = jnp.einsum("esf,edf->esd", d_pre, full_up, preferred_element_type=jnp.float32)
    d_inner = to_tokens(d_inputs).astype(jnp.bfloat16)
    part_down = jnp.einsum("esf,esd->efd", hidden, grads_in, preferred_element_type=jnp.float32)
    part_up = jnp.einsum("esd,esf->edf", inputs, d_pre, preferred_element_type=jnp.float32)
    slots_up = jnp.split(part_up, half, axis=2)
    slots_down = turned(jnp.split(part_down, half, axis=1))
    grad_up = reduce_step(slots_up[1], slots_up, 0, forth)
    grad_down = reduce_step(slots_down[1], slots_down, 0, back)
    d_inner, hidden, grad_up, grad_down = lax.optimization_barrier((d_inner, hidden, grad_up, grad_down))
    grad_up = reduce_step(grad_up, slots_up, 1, forth)
    grad_down = reduce_step(grad_down, slots_down, 1, back)
    resid_grad = norm_back(resid.astype(jnp.float32), d_inner.astype(jnp.float32))
    d_resid = (d_out.astype(jnp.float32) + resid_grad).astype(jnp.bfloat16)
    d_packed, left, right = attention_back(d_resid, col, row, w_o, packed, normed, mixed)
    result = jnp.einsum("esf,efd->esd", hidden, full_down, preferred_element_type=jnp.float32)
    expert_out = to_tokens(result)
    out = (resid.astype(jnp.float32) + expert_out).astype(jnp.bfloat16)
    left_steps, right_steps = halving_steps(False), halving_steps(True)
    parts = (2,) * len(left_steps) + (left.shape[0] // (shards * groups), left.shape[1])
    left, right = left.reshape(parts), right.reshape(parts)
    for number, (one, other) in enumerate(zip(left_steps, right_steps)):
        if number == 1:
            left, right, grad_up, grad_down = lax.optimization_barrier((left, right, grad_up, grad_down))
            for step in range(2, half - 1):
                grad_up = reduce_step(grad_up, slots_up, step, forth)
                grad_down = reduce_step(grad_down, slots_down, step, back)
        left, right = halve(left, *one), halve(right, *other)
    left, right = left.reshape(parts[-2:]), right.reshape(parts[-2:])
    attended = mixed.shape[1]
    grad_qkv = jnp.concatenate([left, right[:, :attended]], axis=1)
    grad_o = right[:, attended:]
    d_normed = col_contract(d_packed, w_qkv).astype(jnp.bfloat16)
    input_grad = norm_back(layer_in.astype(jnp.float32), d_normed.astype(jnp.float32))
    grad_input = (d_resid.astype(jnp.float32) + input_grad).astype(jnp.bfloat16)
    return (out, grad_input, grad_qkv, grad_o, grad_up, grad_down)


def solution(mesh):
    in_specs = (
        P(("dp", "expert"), None),
        P(("dp", "expert")),
        P(("dp", "expert"), None),
        P(),
        P(),
        P("expert", None, "dp"),
        P("expert", "dp", None),
        P(("dp", "expert"), None),
    )
    out_specs = (
        P(("dp", "expert"), None),
        P(("dp", "expert"), None),
        P(("dp", "expert"), None),
        P(("dp", "expert"), None),
        P("expert", None, "dp"),
        P("expert", "dp", None),
    )
    return jax.shard_map(
        on_device, mesh=mesh, in_specs=in_specs, out_specs=out_specs, check_vma=False
    )
```

```python
import jax
import jax.numpy as jnp
from jax import lax
from jax.experimental import pallas as pl
from jax.experimental.pallas import tpu as pltpu
from jax.sharding import PartitionSpec as P

HD = 64


EPSILON = 1e-06


def rms_norm(values):
    scale = lax.rsqrt(jnp.mean(values * values, axis=-1, keepdims=True) + EPSILON)
    return (values * scale).astype(jnp.bfloat16)


def gelu_tanh(values):
    return jax.nn.gelu(values, approximate=True)


def gelu_back(pre_act, cotangent):
    return jax.vjp(gelu_tanh, pre_act)[1](cotangent)[0]


def row_contract(left, right):
    return lax.dot_general(
        left, right, (((0,), (0,)), ((), ())), preferred_element_type=jnp.float32
    )


def col_contract(left, right):
    return lax.dot_general(
        left, right, (((1,), (1,)), ((), ())), preferred_element_type=jnp.float32
    )


def softmax_parts(packed_ref, rows, pair, side, width, same, first):
    query = packed_ref[rows, pl.ds(pair * 128, 128)]
    keys = packed_ref[rows, pl.ds(width + pair * 128, 128)]
    mine = first if side == 0 else jnp.logical_not(first)
    query = jnp.where(mine, query, jnp.zeros_like(query))
    scores = col_contract(query, keys) * HD ** (-0.5)
    weights = jnp.where(same, jnp.exp(scores), 0.0)
    return weights / jnp.sum(weights, axis=-1, keepdims=True)


def first_half():
    return lax.broadcasted_iota(jnp.int32, (128, 128), 1) < HD


def front_kernel(x_ref, col_ref, row_ref, qkv_ref, wo_ref, normed_ref, packed_ref, mixed_ref, resid_ref, inner_ref):
    width = mixed_ref.shape[1]
    first = first_half()
    normed_ref[...] = rms_norm(x_ref[...].astype(jnp.float32))
    packed_ref[...] = jnp.dot(
        normed_ref[...], qkv_ref[...], preferred_element_type=jnp.float32
    ).astype(jnp.bfloat16)
    for block in range(x_ref.shape[0] // 128):
        rows = pl.ds(block * 128, 128)
        same = col_ref[rows, :] == row_ref[:, rows]
        for pair in range(width // 128):
            values = packed_ref[rows, pl.ds(2 * width + pair * 128, 128)]
            heads = []
            for side in range(2):
                probs = softmax_parts(packed_ref, rows, pair, side, width, same, first)
                heads.append(
                    jnp.dot(probs.astype(jnp.bfloat16), values, preferred_element_type=jnp.float32)
                )
            mixed_ref[rows, pl.ds(pair * 128, 128)] = jnp.where(first, heads[0], heads[1]).astype(
                jnp.bfloat16
            )
    resid = (x_ref[...].astype(jnp.float32) + col_contract(mixed_ref[...], wo_ref[...])).astype(
        jnp.bfloat16
    )
    resid_ref[...] = resid
    inner_ref[...] = rms_norm(resid.astype(jnp.float32))


def back_kernel(grad_ref, col_ref, row_ref, wo_ref, packed_ref, normed_ref, mixed_ref, out_ref, left_ref, right_ref, mixed_grad_ref):
    width = wo_ref.shape[1]
    first = first_half()
    mixed_grad_ref[...] = jnp.dot(
        grad_ref[...], wo_ref[...], preferred_element_type=jnp.float32
    ).astype(jnp.bfloat16)
    for block in range(grad_ref.shape[0] // 128):
        rows = pl.ds(block * 128, 128)
        same = col_ref[rows, :] == row_ref[:, rows]
        for pair in range(width // 128):
            query = packed_ref[rows, pl.ds(pair * 128, 128)]
            keys = packed_ref[rows, pl.ds(width + pair * 128, 128)]
            values = packed_ref[rows, pl.ds(2 * width + pair * 128, 128)]
            d_mixed = mixed_grad_ref[rows, pl.ds(pair * 128, 128)]
            parts = []
            for side in range(2):
                mine = first if side == 0 else jnp.logical_not(first)
                probs = softmax_parts(packed_ref, rows, pair, side, width, same, first)
                d_values = row_contract(probs.astype(jnp.bfloat16), d_mixed)
                d_probs = col_contract(jnp.where(mine, d_mixed, jnp.zeros_like(d_mixed)), values)
                d_probs = d_probs.astype(jnp.bfloat16).astype(jnp.float32)
                inside = jnp.sum(d_probs * probs, axis=-1, keepdims=True)
                d_scores = (probs * (d_probs - inside) * HD ** (-0.5)).astype(jnp.bfloat16)
                d_query = jnp.dot(d_scores, keys, preferred_element_type=jnp.float32)
                d_keys = row_contract(d_scores, query)
                parts.append((d_query, d_keys, d_values))
            for at, (left, right) in enumerate(zip(*parts)):
                out_ref[rows, pl.ds(at * width + pair * 128, 128)] = jnp.where(
                    first, left, right
                ).astype(jnp.bfloat16)
    add_terms(grad_ref, normed_ref, mixed_ref, out_ref, left_ref, right_ref)


def add_terms(grad_ref, normed_ref, mixed_ref, out_ref, left_ref, right_ref):
    width = mixed_ref.shape[1]
    left_ref[...] = row_contract(normed_ref[...], out_ref[:, : 2 * width])
    right_ref[:, :width] = row_contract(normed_ref[...], out_ref[:, 2 * width :])
    right_ref[:, width:] = row_contract(grad_ref[...], mixed_ref[...])


def front(x, col, row, w_qkv, w_o):
    rows, width = x.shape[0], w_o.shape[1]
    shape = lambda cols: jax.ShapeDtypeStruct((rows, cols), jnp.bfloat16)
    return pl.pallas_call(
        front_kernel,
        out_shape=[shape(x.shape[1]), shape(3 * width), shape(width), shape(x.shape[1]), shape(x.shape[1])],
        compiler_params=pltpu.CompilerParams(vmem_limit_bytes=40 * 1024 * 1024),
        cost_estimate=pl.CostEstimate(flops=6 * 10**9, bytes_accessed=7 * 10**6, transcendentals=0),
        name="front",
    )(x, col, row, w_qkv, w_o)


def attention_back(d_resid, col, row, w_o, packed, normed, mixed):
    term = jax.ShapeDtypeStruct((normed.shape[1], 2 * mixed.shape[1]), jnp.float32)
    return pl.pallas_call(
        back_kernel,
        out_shape=[jax.ShapeDtypeStruct(packed.shape, jnp.bfloat16), term, term],
        scratch_shapes=[pltpu.VMEM((packed.shape[0], w_o.shape[1]), jnp.bfloat16)],
        compiler_params=pltpu.CompilerParams(vmem_limit_bytes=48 * 1024 * 1024),
        cost_estimate=pl.CostEstimate(flops=6 * 10**9, bytes_accessed=16 * 10**6, transcendentals=0),
        name="attention_back",
    )(d_resid, col, row, w_o, packed, normed, mixed)


def norm_back(values, cotangent):
    scale = lax.rsqrt(jnp.mean(values * values, axis=-1, keepdims=True) + EPSILON)
    along = jnp.mean(values * cotangent, axis=-1, keepdims=True)
    return scale * (cotangent - values * (scale * scale * along))


def stage_perm(count, bit):
    return [(i, i ^ bit) for i in range(count)]


def halve(values, axis_name, count, axis, bit):
    own = (lax.axis_index(axis_name) // bit) % 2
    keep = lax.dynamic_index_in_dim(values, own, axis, keepdims=True)
    give = lax.dynamic_index_in_dim(values, 1 - own, axis, keepdims=True).astype(jnp.bfloat16)
    came = lax.ppermute(give, axis_name, stage_perm(count, bit))
    return keep + came.astype(jnp.float32)


def halving_steps(late_y):
    bits = []
    for name in ("dp", "expert"):
        count = lax.axis_size(name)
        bit = count // 2
        while bit:
            bits.append((name, count, len(bits), bit))
            bit //= 2
    expert_bits = [b for b in reversed(bits) if b[0] == "expert"]
    group_bits = [b for b in reversed(bits) if b[0] == "dp"]
    if late_y:
        return expert_bits[:1] + group_bits[:1] + expert_bits[1:] + group_bits[1:]
    return expert_bits + group_bits


def ring_pairs(groups, step):
    half = groups // 2
    return [(i, ((i // 2 + step) % half) * 2 + i % 2) for i in range(groups)]


def gather_step(slots, pairs):
    return slots + [lax.ppermute(slots[-1], "dp", pairs)]


def turned(slots):
    return slots[:1] + slots[:0:-1]


def reduce_step(total, slots, step, pairs):
    came = lax.ppermute(total.astype(jnp.bfloat16), "dp", pairs)
    return came.astype(jnp.float32) + slots[(step + 2) % len(slots)]


def on_device(layer_in, body_of, expert_of, w_qkv, w_o, w_up, w_down, d_out):
    tok_rows = layer_in.shape[0]
    width = layer_in.shape[1]
    shards = lax.axis_size("expert")
    groups = lax.axis_size("dp")
    half = groups // 2
    local_experts = w_up.shape[0]
    all_experts = local_experts * shards
    capacity = 3 * tok_rows // (2 * all_experts)
    received = shards * capacity
    partner = stage_perm(groups, 1)
    forth, back = ring_pairs(groups, 1), ring_pairs(groups, -1)

    ups, downs = gather_step([w_up], forth), gather_step([w_down], back)

    ids = expert_of[:, 0]
    at = jnp.arange(tok_rows, dtype=jnp.int32)
    earlier = (ids[:, None] == ids[None, :]) & (at[None, :] < at[:, None])
    ranks = jnp.sum(earlier.astype(jnp.int32), axis=1)
    slots = ids * capacity + ranks
    places = jnp.arange(all_experts * capacity, dtype=jnp.int32)
    spread = (places[:, None] == slots[None, :]).astype(jnp.bfloat16)

    def to_slots(values):
        store = jnp.dot(spread, values, preferred_element_type=jnp.float32).astype(jnp.bfloat16)
        return store.reshape(shards, local_experts, capacity, width)

    def exchange(store):
        sent = lax.all_to_all(store, "expert", split_axis=0, concat_axis=2, tiled=True)
        return sent.reshape(local_experts, received, width)

    def with_partner(own):
        return jnp.concatenate([own, lax.ppermute(own, "dp", partner)], axis=1)

    def to_tokens(values):
        other = lax.ppermute(values[:, received:].astype(jnp.bfloat16), "dp", partner)
        total = (values[:, :received] + other.astype(jnp.float32)).astype(jnp.bfloat16)
        total = total.reshape(local_experts, shards, capacity, width)
        returned = lax.all_to_all(total, "expert", split_axis=1, concat_axis=0, tiled=True)
        returned = returned.reshape(all_experts * capacity, width)
        return row_contract(spread, returned)

    col, row = body_of[:, None], body_of[None, :]
    store, layer_in = lax.optimization_barrier((to_slots(d_out), layer_in))
    own_grads = exchange(store)
    normed, packed, mixed, resid, inner = front(layer_in, col, row, w_qkv, w_o)
    own_inputs = exchange(to_slots(inner))
    own_inputs, own_grads, ups, downs = lax.optimization_barrier((own_inputs, own_grads, ups, downs))
    ups, downs = gather_step(ups, forth), gather_step(downs, back)
    inputs, grads_in = with_partner(own_inputs), with_partner(own_grads)
    inputs, ups, downs = lax.optimization_barrier((inputs, ups, downs))
    while len(ups) < half:
        ups, downs = gather_step(ups, forth), gather_step(downs, back)
    full_up = jnp.concatenate(ups, axis=2)
    full_down = jnp.concatenate(turned(downs), axis=1)
    d_hidden = jnp.einsum("esd,efd->esf", grads_in, full_down, preferred_element_type=jnp.float32)
    pre_act = jnp.einsum("esd,edf->esf", inputs, full_up, preferred_element_type=jnp.float32)
    hidden = gelu_tanh(pre_act).astype(jnp.bfloat16)
    d_pre = gelu_back(pre_act, d_hidden).astype(jnp.bfloat16)
    d_inputs = jnp.einsum("esf,edf->esd", d_pre, full_up, preferred_element_type=jnp.float32)
    d_inner = to_tokens(d_inputs).astype(jnp.bfloat16)
    part_down = jnp.einsum("esf,esd->efd", hidden, grads_in, preferred_element_type=jnp.float32)
    part_up = jnp.einsum("esd,esf->edf", inputs, d_pre, preferred_element_type=jnp.float32)
    slots_up = jnp.split(part_up, half, axis=2)
    slots_down = turned(jnp.split(part_down, half, axis=1))
    grad_up = reduce_step(slots_up[1], slots_up, 0, forth)
    grad_down = reduce_step(slots_down[1], slots_down, 0, back)
    d_inner, hidden, grad_up, grad_down = lax.optimization_barrier((d_inner, hidden, grad_up, grad_down))
    grad_up = reduce_step(grad_up, slots_up, 1, forth)
    grad_down = reduce_step(grad_down, slots_down, 1, back)
    resid_grad = norm_back(resid.astype(jnp.float32), d_inner.astype(jnp.float32))
    d_resid = (d_out.astype(jnp.float32) + resid_grad).astype(jnp.bfloat16)
    d_packed, left, right = attention_back(d_resid, col, row, w_o, packed, normed, mixed)
    result = jnp.einsum("esf,efd->esd", hidden, full_down, preferred_element_type=jnp.float32)
    expert_out = to_tokens(result)
    out = (resid.astype(jnp.float32) + expert_out).astype(jnp.bfloat16)
    left_steps, right_steps = halving_steps(False), halving_steps(True)
    parts = (2,) * len(left_steps) + (left.shape[0] // (shards * groups), left.shape[1])
    left, right = left.reshape(parts), right.reshape(parts)
    for number, (one, other) in enumerate(zip(left_steps, right_steps)):
        if number == 1:
            left, right, grad_up, grad_down = lax.optimization_barrier((left, right, grad_up, grad_down))
            for step in range(2, half - 1):
                grad_up = reduce_step(grad_up, slots_up, step, forth)
                grad_down = reduce_step(grad_down, slots_down, step, back)
        left, right = halve(left, *one), halve(right, *other)
    left, right = left.reshape(parts[-2:]), right.reshape(parts[-2:])
    attended = mixed.shape[1]
    grad_qkv = jnp.concatenate([left, right[:, :attended]], axis=1)
    grad_o = right[:, attended:]
    d_normed = col_contract(d_packed, w_qkv).astype(jnp.bfloat16)
    input_grad = norm_back(layer_in.astype(jnp.float32), d_normed.astype(jnp.float32))
    grad_input = (d_resid.astype(jnp.float32) + input_grad).astype(jnp.bfloat16)
    return (out, grad_input, grad_qkv, grad_o, grad_up, grad_down)


def solution(mesh):
    in_specs = (
        P(("dp", "expert"), None),
        P(("dp", "expert")),
        P(("dp", "expert"), None),
        P(),
        P(),
        P("expert", None, "dp"),
        P("expert", "dp", None),
        P(("dp", "expert"), None),
    )
    out_specs = (
        P(("dp", "expert"), None),
        P(("dp", "expert"), None),
        P(("dp", "expert"), None),
        P(("dp", "expert"), None),
        P("expert", None, "dp"),
        P("expert", "dp", None),
    )
    return jax.shard_map(
        on_device, mesh=mesh, in_specs=in_specs, out_specs=out_specs, check_vma=False
    )
```
